128 devices in a mesh: adapter: 16 (over x, z), tensor: 8 (over y, core).
Axes of the slice: x: 4, y: 4, z: 4, core: 2. Of those that a mesh axis runs over, the one named last changes fastest.
Arguments:
- tokens: bfloat16 [8192, 8192], P(('adapter', 'tensor')), may hold values from -6 to 6
- token_adapter_index: int32 [8192], P(('adapter', 'tensor')), may hold values from 0 to 1023, as said below
- joined_weight_matrix: bfloat16 [8192, 10240], P(None, 'tensor'), may hold values from -0.0625 to 0.0625
- adapter_down_weight: bfloat16 [1024, 16, 8192], P('adapter', None, 'tensor'), may hold values from -0.0625 to 0.0625
- adapter_up_weight: bfloat16 [1024, 16, 10240], P('adapter', None, 'tensor'), may hold values from -0.75 to 0.75
Outputs:
- projected: bfloat16 [8192, 10240], P('adapter', 'tensor')
The draws below stay inside these ranges and needn't reach their ends.
Inputs may be any that keep to these rules, and one draw needn't show every extreme that they name: `token_adapter_index`: in every aligned block of 512 rows, at most 128 rows name adapters of one owner, owner o holding adapters o * 64 to (o + 1) * 64 - 1; one owner gets exactly 128 rows of every block.
All inputs are finite; a program needn't handle non-finite values.
Results may differ from the reference program's by a relative error of at most 0.0049.
Values may be sent and summed in bfloat16 or wider, within the bound.
No kernel may reach another device: no remote copies, remote signals or barrier semaphores. Data moves between devices by JAX's collectives and lax.ppermute only.
A program may use at most 128 MiB of HBM per device.

```python
import jax
import jax.numpy as jnp
from jax import lax

MODEL_WIDTH = 8192
QUERY_KEY_VALUE = 10240
ADAPTER_RANK = 16
ADP_DEV = 64
ADAPTER_TOTAL = 1024
GROUP = 512
TOKENS = 8192
CAP = 128


def draw_token_adapter_index(key, part):
    key = jax.random.fold_in(key, 11)
    key_hot, key_start, key_perm, key_local = jax.random.split(key, 4)
    blocks = TOKENS // GROUP
    owners = blocks
    hot = jax.random.randint(key_hot, (), 0, owners)
    start = jax.random.randint(key_start, (blocks, 1), 0, owners - 1)
    position = jnp.arange(GROUP, dtype=jnp.int32)[None, :]
    offset = (position - CAP + start) % (owners - 1)
    other = (hot + 1 + offset) % owners
    owner = jnp.where(position < CAP, hot, other)
    perms = jax.vmap(lambda single: jax.random.permutation(single, GROUP))(jax.random.split(key_perm, blocks))
    owner = jnp.take_along_axis(owner, perms, axis=1)
    local = jax.random.randint(key_local, (blocks, GROUP), 0, ADP_DEV)
    return (owner * ADP_DEV + local).reshape(TOKENS).astype(jnp.int32)


def block_levels(own_key, dims, shards, low, high):
    def one(axis_at, blocks):
        steps = jax.random.uniform(jax.random.fold_in(jax.random.fold_in(own_key, 6), axis_at), (blocks,), jnp.float32, low / len(shards), high / len(shards))
        return jnp.repeat(jnp.exp(steps), dims[axis_at] // blocks).reshape((-1,) + (1,) * (len(dims) - axis_at - 1))

    loudness = one(*shards[0])
    for cut in shards[1:]:
        loudness = loudness * one(*cut)
    return loudness


def gaussian(own_key, extent, spread, limit, cuts=(), held_as=jnp.bfloat16):
    drawn = jax.random.normal(own_key, extent, jnp.float32) * spread
    if len(cuts) > 0:
        drawn = block_levels(own_key, extent, cuts, -0.22, 0.18) * drawn
    return jnp.clip(drawn, min=-limit, max=limit).astype(held_as)


def setup_inputs(seed: int = 0) -> dict:
    seeds = jax.random.split(jax.random.key(seed), 6)
    tokens = gaussian(seeds[0], (TOKENS, MODEL_WIDTH), 1.0, 6.0, ((0, 128),))
    token_adapter_index = draw_token_adapter_index(jax.random.fold_in(seeds[5], 71), 0)
    joined_weight_matrix = gaussian(seeds[2], (MODEL_WIDTH, QUERY_KEY_VALUE), MODEL_WIDTH ** -0.5, 0.0625, ((1, 8),))
    adapter_down_weight = gaussian(seeds[3], (ADAPTER_TOTAL, ADAPTER_RANK, MODEL_WIDTH), MODEL_WIDTH ** -0.5, 0.0625, ((0, 16), (2, 8)))
    adapter_up_weight = gaussian(seeds[4], (ADAPTER_TOTAL, ADAPTER_RANK, QUERY_KEY_VALUE), (4 * ADAPTER_RANK) ** -0.5, 0.75, ((0, 16), (2, 8)))
    return dict(tokens=tokens, token_adapter_index=token_adapter_index, joined_weight_matrix=joined_weight_matrix, adapter_down_weight=adapter_down_weight, adapter_up_weight=adapter_up_weight)


def reference(tokens, token_adapter_index, joined_weight_matrix, adapter_down_weight, adapter_up_weight):
    base = jnp.dot(tokens, joined_weight_matrix, preferred_element_type=jnp.float32)
    blocks = TOKENS // GROUP

    def one_block(operands):
        rows, adapter_index = operands
        down_matrix = adapter_down_weight[adapter_index].astype(jnp.float32)
        low = jnp.einsum("gd,grd->gr", rows.astype(jnp.float32), down_matrix)
        low = low.astype(jnp.bfloat16).astype(jnp.float32)
        up_matrix = adapter_up_weight[adapter_index].astype(jnp.float32)
        delta = 2.0 * jnp.einsum("gr,grc->gc", low, up_matrix)
        return delta.astype(jnp.bfloat16)

    deltas = lax.map(one_block, (tokens.reshape(blocks, GROUP, MODEL_WIDTH), token_adapter_index.reshape(blocks, GROUP)))
    deltas = deltas.reshape(TOKENS, QUERY_KEY_VALUE)
    return (base + deltas.astype(jnp.float32)).astype(jnp.bfloat16)
```

```python
import functools

import jax
import jax.numpy as jnp
from jax import lax
from jax.experimental import pallas as pl
from jax.experimental.pallas import tpu as pltpu
from jax.sharding import PartitionSpec as P

BF16, F32, I32 = jnp.bfloat16, jnp.float32, jnp.int32
LANES = 128
VMEM = pl.BlockSpec(memory_space=pltpu.VMEM)
LIMIT = 48 * 1024 * 1024


def iota(shape, dim):
    return lax.broadcasted_iota(I32, shape, dim)


def rows_by_rows(a, b):
    return lax.dot_general(a, b, (((1,), (1,)), ((), ())), preferred_element_type=F32)


def columns_by_columns(a, b):
    return lax.dot_general(a, b, (((0,), (0,)), ((), ())), preferred_element_type=F32)


def lane_as_row(extra, lane):
    pick = (iota((8, LANES), 1) == lane).astype(BF16)
    return rows_by_rows(pick, extra).astype(I32)


def route_kernel(owners, even, rest, slab_ref, main_ref, rest_ref, info_ref, rows_ref):
    members, local_rows, wide = slab_ref.shape
    group = members * local_rows
    for i in range(members):
        rows_ref[pl.ds(i * local_rows, local_rows), :] = slab_ref[i]
    extra = rows_ref[:, wide - LANES :]
    owner = lane_as_row(extra, 0)
    local = lane_as_row(extra, 1)
    hot = iota((owners, group), 0) == owner[0:1]
    hot16 = hot.astype(BF16)
    earlier = (iota((group, group), 0) < iota((group, group), 1)).astype(BF16)
    before = jnp.dot(hot16, earlier, preferred_element_type=F32)
    place = jnp.sum(jnp.where(hot, before, 0.0), axis=0, keepdims=True).astype(I32)
    counts = jnp.sum(jnp.where(hot, 1, 0), axis=1, keepdims=True)
    most = jnp.max(counts, axis=0, keepdims=True)
    number = iota((owners, 1), 0)
    full = jnp.min(jnp.where(counts == most, number, owners), axis=0, keepdims=True)
    others = jnp.max(jnp.where(number == full, 0, counts), axis=0, keepdims=True)

    target = jnp.where(place < even, owner[0:1] * even + place, -1)
    send = jnp.dot(
        (iota((owners * even, group), 0) == target).astype(BF16),
        rows_ref[...],
        preferred_element_type=F32,
    )
    tail = send[:, wide - LANES :]
    lane = iota(tail.shape, 1)
    tail = jnp.where(lane == 2, full.astype(F32), tail)
    tail = jnp.where(lane == 3, others.astype(F32), tail)
    tail = jnp.where(lane == 4, most.astype(F32), tail)
    main_ref[:, : wide - LANES] = send[:, : wide - LANES].astype(BF16)
    main_ref[:, wide - LANES :] = tail.astype(BF16)

    spare = jnp.where((owner[0:1] == full) & (place >= even), place - even, -1)
    rest_ref[...] = jnp.dot(
        (iota((rest, group), 0) == spare).astype(BF16), rows_ref[...], preferred_element_type=F32
    ).astype(BF16)
    line = iota((8, group), 0)
    info_ref[...] = jnp.where(line == 0, owner, jnp.where(line == 1, local, place))


def route(slab, owners, even, rest):
    members, local_rows, wide = slab.shape
    group = members * local_rows
    return pl.pallas_call(
        functools.partial(route_kernel, owners, even, rest),
        out_shape=(
            jax.ShapeDtypeStruct((owners * even, wide), BF16),
            jax.ShapeDtypeStruct((rest, wide), BF16),
            jax.ShapeDtypeStruct((8, group), I32),
        ),
        in_specs=[VMEM],
        out_specs=(VMEM, VMEM, VMEM),
        scratch_shapes=[pltpu.VMEM((group, wide), BF16)],
        compiler_params=pltpu.CompilerParams(vmem_limit_bytes=LIMIT),
        name="route",
    )(slab)


def low_kernel(rank, rows_ref, down_ref, low_ref, local_ref):
    features = down_ref.shape[1]
    held = down_ref.shape[0] // rank
    wide = rows_by_rows(down_ref[...], rows_ref[:, :features])
    local = lane_as_row(rows_ref[:, features:], 1)
    local_ref[...] = local
    total = jnp.zeros(low_ref.shape, F32)
    for i in range(held):
        total += jnp.where(local[0:1] == i, wide[i * rank : (i + 1) * rank], 0.0)
    low_ref[...] = total


def low_part(rows, down, rank, tile):
    count, wide = rows.shape
    return pl.pallas_call(
        functools.partial(low_kernel, rank),
        grid=(count // tile,),
        in_specs=[
            pl.BlockSpec((tile, wide), lambda i: (i, 0)),
            pl.BlockSpec(down.shape, lambda i: (0, 0)),
        ],
        out_specs=(
            pl.BlockSpec((rank, tile), lambda i: (0, i)),
            pl.BlockSpec((8, tile), lambda i: (0, i)),
        ),
        out_shape=(
            jax.ShapeDtypeStruct((rank, count), F32),
            jax.ShapeDtypeStruct((8, count), I32),
        ),
        compiler_params=pltpu.CompilerParams(vmem_limit_bytes=LIMIT),
        cost_estimate=pl.CostEstimate(
            flops=2 * count * down.shape[0] * down.shape[1],
            bytes_accessed=2 * (rows.size + down.size),
            transcendentals=0,
        ),
        name="low",
    )(rows, down)


def spread(low, local, held):
    none = jnp.zeros_like(low)
    return jnp.concatenate([jnp.where(local == i, low, none) for i in range(held)], axis=0)


def delta_kernel(low_ref, local_ref, up_ref, out_ref):
    held = up_ref.shape[0] // low_ref.shape[0]
    chosen = spread(low_ref[...], local_ref[0:1], held)
    out_ref[...] = (2.0 * columns_by_columns(chosen, up_ref[...])).astype(BF16)


def delta_of(low, local, up):
    count, columns = low.shape[1], up.shape[1]
    return pl.pallas_call(
        delta_kernel,
        out_shape=jax.ShapeDtypeStruct((count, columns), BF16),
        in_specs=[VMEM] * 3,
        out_specs=VMEM,
        compiler_params=pltpu.CompilerParams(vmem_limit_bytes=LIMIT),
        cost_estimate=pl.CostEstimate(
            flops=2 * count * up.size, bytes_accessed=2 * (up.size + count * columns), transcendentals=0
        ),
        name="delta",
    )(low, local, up)


def finish_kernel(even, full_ref, info_ref, low_ref, base_ref, back_ref, up_ref, out_ref):
    slots = back_ref.shape[0]
    rank, spare_slots = low_ref.shape
    held = up_ref.shape[0] // rank
    group = info_ref.shape[1]
    owner, local, place = info_ref[0:1], info_ref[1:2], info_ref[2:3]
    target = jnp.where(place < even, owner * even + place, -1)
    chosen = (iota((slots, group), 0) == target).astype(BF16)
    spare = jnp.where((owner == full_ref[0]) & (place >= even), place - even, -1)
    chosen_spare = (iota((spare_slots, group), 0) == spare).astype(BF16)
    local_rows = jnp.broadcast_to(local, (8, group)).astype(F32).astype(BF16)
    local_spare = rows_by_rows(local_rows, chosen_spare).astype(I32)
    wide = spread(low_ref[...], local_spare[0:1], held)
    delta = (2.0 * columns_by_columns(wide, up_ref[...])).astype(BF16)
    total = base_ref[...] + columns_by_columns(chosen, back_ref[...])
    out_ref[...] = (total + columns_by_columns(chosen_spare, delta)).astype(BF16)


def finish(full, info, low, base, back, up, even, tile):
    group, columns = base.shape
    whole = lambda a: pl.BlockSpec(a.shape, lambda i: (0, 0))
    cut = lambda a: pl.BlockSpec((a.shape[0], tile), lambda i: (0, i))
    return pl.pallas_call(
        functools.partial(finish_kernel, even),
        grid=(columns // tile,),
        in_specs=[
            pl.BlockSpec(memory_space=pltpu.SMEM),
            whole(info),
            whole(low),
            cut(base),
            cut(back),
            cut(up),
        ],
        out_specs=pl.BlockSpec((group, tile), lambda i: (0, i)),
        out_shape=jax.ShapeDtypeStruct((group, columns), BF16),
        compiler_params=pltpu.CompilerParams(vmem_limit_bytes=LIMIT),
        name="finish",
    )(full, info, low, base, back, up)


def exchange(block, axis):
    return lax.all_to_all(block, axis, split_axis=0, concat_axis=0, tiled=True)


def shifted(block, step):
    members = lax.axis_size("tensor")
    return lax.ppermute(block, "tensor", [(i, (i + step) % members) for i in range(members)])


def swapped(block, bit):
    members = lax.axis_size("tensor")
    return lax.ppermute(block, "tensor", [(i, i ^ bit) for i in range(members)])


def total_over_tensor(part):
    for bit in (1, 2, 4):
        part = part + swapped(part, bit)
    return part


def gather_rows(own):
    rows = own.shape[0]
    half = rows // 2
    before = shifted(own, 2)
    after = shifted(own, -2)
    across = jnp.concatenate([shifted(before[:half], 2), shifted(after[half:], -2)], axis=0)
    here = lax.axis_index("tensor")
    chip, core = here // 2, here % 2
    full = jnp.zeros((8 * rows, own.shape[1]), own.dtype)
    for away, block in ((0, own), (3, before), (1, after), (2, across)):
        other = swapped(block, 1)
        start = ((chip + away) % 4) * 2 * rows
        full = lax.dynamic_update_slice(full, block, (start + core * rows, 0))
        full = lax.dynamic_update_slice(full, other, (start + (1 - core) * rows, 0))
    return full


def per_device(
    tokens, token_adapter_index, joined_weight_matrix, adapter_down_weight, adapter_up_weight
):
    owners = lax.axis_size("adapter")
    members = lax.axis_size("tensor")
    local_rows, width = tokens.shape
    group = members * local_rows
    held, rank, features = adapter_down_weight.shape
    columns = adapter_up_weight.shape[2]
    capacity = 4 * group // owners
    even = group // owners
    rest = capacity - even
    down = adapter_down_weight.reshape(held * rank, features)
    up = adapter_up_weight.reshape(held * rank, columns)
    wide = features + LANES

    numbers = jnp.stack([token_adapter_index // held, token_adapter_index % held], axis=1)
    numbers = jnp.pad(numbers.astype(BF16), ((0, 0), (0, LANES - 2)))
    blocks = tokens.reshape(local_rows, members, features).transpose(1, 0, 2)
    numbers = jnp.broadcast_to(numbers[None], (members, local_rows, LANES))
    slab = exchange(jnp.concatenate([blocks, numbers], axis=2), "tensor")

    send, send_rest, info = route(slab, owners, even, rest)
    rest_rows = lax.all_gather(send_rest, "adapter", axis=0, tiled=True)
    rows = exchange(send.reshape(owners, even, wide), "adapter")

    said = rows[:, 0, features + 2 : features + 5].astype(I32)
    same = jnp.all(said[:, 0] == said[0, 0])
    full = jnp.where(same, said[0, 0], -1)
    largest = jnp.where(same, jnp.max(said[:, 1]), jnp.max(said[:, 2]))
    turns = (largest + even - 1) // even

    pieces = exchange(up.reshape(owners, up.shape[0] // owners, columns), "adapter")
    piece = lax.dynamic_index_in_dim(pieces, jnp.maximum(full, 0), 0, keepdims=False)
    up_full = lax.all_gather(piece, "adapter", axis=0, tiled=True)

    part, local = low_part(rows.reshape(owners * even, wide), down, rank, owners * even)
    low = total_over_tensor(part).astype(BF16)
    delta = delta_of(low, local, up)
    back = exchange(delta.reshape(owners, even, columns), "adapter").reshape(owners * even, columns)

    rest_part, _ = low_part(rest_rows, down, rank, owners * rest // 3)
    rest_low = total_over_tensor(rest_part).astype(BF16).reshape(rank, owners, rest)
    rest_low = jnp.pad(rest_low.transpose(1, 0, 2), ((0, 0), (0, 0), (0, capacity - rest)))
    low_back = exchange(rest_low, "adapter")
    low_full = lax.dynamic_index_in_dim(low_back, jnp.maximum(full, 0), 0, keepdims=False)

    ready, _ = lax.optimization_barrier((tokens, send))
    base = jnp.dot(gather_rows(ready), joined_weight_matrix, preferred_element_type=F32)

    owner, place = info[0], info[2]
    flat = slab.reshape(group, wide)

    def more(carry):
        turn, total = carry
        wanted = (owner != full) & (place // even == turn)
        slot = jnp.where(wanted, owner * even + place % even, -1)
        chosen = (slot[None, :] == jnp.arange(owners * even, dtype=I32)[:, None]).astype(BF16)
        moved = jnp.dot(chosen, flat, preferred_element_type=F32).astype(BF16)
        moved = exchange(moved.reshape(owners, even, wide), "adapter").reshape(owners * even, wide)
        more_part, more_local = low_part(moved, down, rank, owners * even)
        more_low = total_over_tensor(more_part).astype(BF16)
        more_delta = delta_of(more_low, more_local, up).reshape(owners, even, columns)
        more_back = exchange(more_delta, "adapter").reshape(owners * even, columns)
        return turn + 1, total + jnp.dot(chosen.T, more_back, preferred_element_type=F32)

    _, base = lax.while_loop(lambda carry: carry[0] < turns, more, (jnp.int32(1), base))
    return finish(full.reshape(1), info, low_full, base, back, up_full, even, 256)


def solution(mesh):
    return jax.shard_map(
        per_device,
        mesh=mesh,
        in_specs=(
            P(("adapter", "tensor"), None),
            P(("adapter", "tensor")),
            P(None, "tensor"),
            P("adapter", None, "tensor"),
            P("adapter", None, "tensor"),
        ),
        out_specs=P("adapter", "tensor"),
        check_vma=False,
    )
```

```python
import functools

import jax
import jax.numpy as jnp
from jax import lax
from jax.experimental import pallas as pl
from jax.experimental.pallas import tpu as pltpu
from jax.sharding import PartitionSpec as P

BF16, F32, I32 = jnp.bfloat16, jnp.float32, jnp.int32
LANES = 128
VMEM = pl.BlockSpec(memory_space=pltpu.VMEM)
LIMIT = 60 * 1024 * 1024
SMALL = 24 * 1024 * 1024


def iota(shape, dim):
    return lax.broadcasted_iota(I32, shape, dim)


def rows_by_rows(a, b):
    return lax.dot_general(a, b, (((1,), (1,)), ((), ())), preferred_element_type=F32)


def columns_by_columns(a, b):
    return lax.dot_general(a, b, (((0,), (0,)), ((), ())), preferred_element_type=F32)


def lane_as_row(extra, lane):
    pick = (iota((8, LANES), 1) == lane).astype(BF16)
    return rows_by_rows(pick, extra).astype(I32)


def plan_kernel(owners, held, even, ids_ref, info_ref, down_ref):
    group = ids_ref.shape[1]
    ids = ids_ref[...]
    owner = ids // held
    hot = iota((owners, group), 0) == owner[0:1]
    earlier = (iota((group, group), 0) < iota((group, group), 1)).astype(BF16)
    before = jnp.dot(hot.astype(BF16), earlier, preferred_element_type=F32)
    place = jnp.sum(jnp.where(hot, before, 0.0), axis=0, keepdims=True).astype(I32)
    counts = jnp.sum(jnp.where(hot, 1, 0), axis=1, keepdims=True)
    most = jnp.max(counts, axis=0, keepdims=True)
    number = iota((owners, 1), 0)
    full = jnp.min(jnp.where(counts == most, number, owners), axis=0, keepdims=True)
    others = jnp.max(jnp.where(number == full, 0, counts), axis=0, keepdims=True)
    info = jnp.broadcast_to(most, (8, group))
    line = iota((8, group), 0)
    for i, value in enumerate((owner, ids - owner * held, place, full, others)):
        info = jnp.where(line == i, value, info)
    info_ref[...] = info
    tall = jnp.concatenate([info.astype(F32), jnp.zeros((LANES - 8, group), F32)], axis=0)
    down_ref[...] = tall.T.astype(I32)


def plan(ids, owners, held, even):
    return pl.pallas_call(
        functools.partial(plan_kernel, owners, held, even),
        out_shape=(
            jax.ShapeDtypeStruct((8, ids.shape[0]), I32),
            jax.ShapeDtypeStruct((ids.shape[0], LANES), I32),
        ),
        in_specs=[VMEM],
        out_specs=(VMEM, VMEM),
        compiler_params=pltpu.CompilerParams(vmem_limit_bytes=SMALL),
        name="plan",
    )(jnp.broadcast_to(ids[None], (8, ids.shape[0])))


def route_kernel(owners, even, at_ref, info_ref, rows_ref, main_ref, rest_ref):
    group, features = rows_ref.shape
    slots, spare_slots = main_ref.shape[0], rest_ref.shape[0]
    info = info_ref[...]
    owner, local, place, full = info[0:1], info[1:2], info[2:3], info[3:4]
    rows = rows_ref[...]
    numbers = jnp.where(iota((LANES, group), 0) == 1, local, 0).astype(F32).astype(BF16)

    target = jnp.where(place < even, owner * even + place, -1)
    chosen = (iota((slots, group), 0) == target).astype(BF16)
    main_ref[:, :features] = jnp.dot(chosen, rows, preferred_element_type=F32).astype(BF16)
    tail = rows_by_rows(chosen, numbers)
    lane = iota(tail.shape, 1)
    for i in (3, 4, 5):
        tail = jnp.where(lane == i, info[i : i + 1, 0:1].astype(F32), tail)
    main_ref[:, features:] = tail.astype(BF16)

    spare = jnp.where((owner == full) & (place >= even), place - even, -1)
    chosen = (iota((spare_slots, group), 0) == spare).astype(BF16)
    rest_ref[:, :features] = jnp.dot(chosen, rows, preferred_element_type=F32).astype(BF16)
    rest_ref[:, features:] = rows_by_rows(chosen, numbers).astype(BF16)


def route(at, info, gathered, features, owners, even, spare_slots):
    group = gathered.shape[0]
    wide = features + LANES
    return pl.pallas_call(
        functools.partial(route_kernel, owners, even),
        grid_spec=pltpu.PrefetchScalarGridSpec(
            num_scalar_prefetch=1,
            grid=(1,),
            in_specs=[
                pl.BlockSpec((8, group), lambda i, at: (0, 0)),
                pl.BlockSpec((group, features), lambda i, at: (0, at[0])),
            ],
            out_specs=(
                pl.BlockSpec((owners * even, wide), lambda i, at: (0, 0)),
                pl.BlockSpec((spare_slots, wide), lambda i, at: (0, 0)),
            ),
        ),
        out_shape=(
            jax.ShapeDtypeStruct((owners * even, wide), BF16),
            jax.ShapeDtypeStruct((spare_slots, wide), BF16),
        ),
        compiler_params=pltpu.CompilerParams(vmem_limit_bytes=SMALL),
        name="route",
    )(at, info, gathered)


def low_kernel(rank, labels_ref, rows_ref, extra_ref, down_ref, low_ref, local_ref):
    step = pl.program_id(0)
    some = down_ref.shape[0] // rank
    local = lane_as_row(extra_ref[...], 1)
    wide = rows_by_rows(down_ref[...], rows_ref[...])
    total = jnp.zeros(low_ref.shape, F32)
    for i in range(some):
        label = labels_ref[step * some + i]
        total += jnp.where(local[0:1] == label, wide[i * rank : (i + 1) * rank], 0.0)

    @pl.when(step == 0)
    def _():
        local_ref[...] = local
        low_ref[...] = total

    @pl.when(step != 0)
    def _():
        low_ref[...] += total


def low_part(labels, rows, down, rank, limit):
    count, wide = rows.shape
    features = wide - LANES
    steps = 4
    return pl.pallas_call(
        functools.partial(low_kernel, rank),
        grid=(steps,),
        in_specs=[
            pl.BlockSpec(memory_space=pltpu.SMEM),
            pl.BlockSpec((count, features), lambda i: (0, 0)),
            pl.BlockSpec((count, LANES), lambda i: (0, features // LANES)),
            pl.BlockSpec((down.shape[0] // steps, features), lambda i: (i, 0)),
        ],
        out_specs=(
            pl.BlockSpec((rank, count), lambda i: (0, 0)),
            pl.BlockSpec((8, count), lambda i: (0, 0)),
        ),
        out_shape=(
            jax.ShapeDtypeStruct((rank, count), F32),
            jax.ShapeDtypeStruct((8, count), I32),
        ),
        compiler_params=pltpu.CompilerParams(vmem_limit_bytes=limit),
        cost_estimate=pl.CostEstimate(
            flops=2 * count * down.shape[0] * features,
            bytes_accessed=2 * features * (count + down.shape[0]),
            transcendentals=0,
        ),
        name="low",
    )(labels, rows, rows, down)


def spread(low, local, labels):
    rank, places = low.shape[0], labels.shape[1]
    repeat = (iota((rank, places), 1) % rank == iota((rank, places), 0)).astype(BF16)
    values = columns_by_columns(low, repeat)
    return jnp.where(local == labels, values, 0.0).astype(BF16)


def delta_kernel(low_ref, extra_ref, up_ref, out_ref, wide_ref):
    rank, places = low_ref.shape[0], up_ref.shape[0]

    @pl.when(pl.program_id(0) == 0)
    def _():
        local = extra_ref[:, 1:2].astype(F32).astype(I32)
        wide_ref[...] = spread(low_ref[...], local, iota((1, places), 1) // rank)

    out_ref[...] = (2.0 * jnp.dot(wide_ref[...], up_ref[...], preferred_element_type=F32)).astype(BF16)


def delta_of(low, rows, up, tile):
    count, wide = rows.shape
    places, columns = up.shape
    return pl.pallas_call(
        delta_kernel,
        grid=(columns // tile,),
        in_specs=[
            pl.BlockSpec(low.shape, lambda i: (0, 0)),
            pl.BlockSpec((count, LANES), lambda i: (0, wide // LANES - 1)),
            pl.BlockSpec((places, tile), lambda i: (0, i)),
        ],
        out_specs=pl.BlockSpec((count, tile), lambda i: (0, i)),
        out_shape=jax.ShapeDtypeStruct((count, columns), BF16),
        scratch_shapes=[pltpu.VMEM((count, places), BF16)],
        compiler_params=pltpu.CompilerParams(vmem_limit_bytes=SMALL),
        cost_estimate=pl.CostEstimate(
            flops=2 * count * up.size, bytes_accessed=2 * (up.size + count * columns), transcendentals=0
        ),
        name="delta",
    )(low, rows, up)


def finish_kernel(
    even,
    full_ref,
    labels_ref,
    tall_ref,
    low_ref,
    extra_ref,
    base_ref,
    back_ref,
    up_ref,
    out_ref,
    wide_ref,
    main_ref,
    rest_ref,
):
    @pl.when(pl.program_id(0) == 0)
    def _():
        owner, place = tall_ref[:, 0:1], tall_ref[:, 2:3]
        target = jnp.where(place < even, owner * even + place, -1)
        main_ref[...] = (iota(main_ref.shape, 1) == target).astype(BF16)
        spare = jnp.where((owner == full_ref[0]) & (place >= even), place - even, -1)
        rest_ref[...] = (iota(rest_ref.shape, 1) == spare).astype(BF16)
        local = extra_ref[:, 1:2].astype(F32).astype(I32)
        wide_ref[...] = spread(low_ref[...], local, labels_ref[0:1])

    delta = (2.0 * jnp.dot(wide_ref[...], up_ref[...], preferred_element_type=F32)).astype(BF16)
    total = base_ref[...] + jnp.dot(main_ref[...], back_ref[...], preferred_element_type=F32)
    total += jnp.dot(rest_ref[...], delta, preferred_element_type=F32)
    out_ref[...] = total.astype(BF16)


def finish(full, labels, tall, low, rows, base, back, weights, even, tile):
    group, columns = base.shape
    skip = (weights.shape[1] - columns) // tile
    whole = lambda a: pl.BlockSpec(a.shape, lambda i: (0, 0))
    cut = lambda a: pl.BlockSpec((a.shape[0], tile), lambda i: (0, i))
    return pl.pallas_call(
        functools.partial(finish_kernel, even),
        grid=(columns // tile,),
        in_specs=[
            pl.BlockSpec(memory_space=pltpu.SMEM),
            whole(labels),
            whole(tall),
            whole(low),
            pl.BlockSpec((rows.shape[0], LANES), lambda i: (0, rows.shape[1] // LANES - 1)),
            cut(base),
            cut(back),
            pl.BlockSpec((weights.shape[0], tile), lambda i: (0, i + skip)),
        ],
        out_specs=pl.BlockSpec((group, tile), lambda i: (0, i)),
        out_shape=jax.ShapeDtypeStruct((group, columns), BF16),
        scratch_shapes=[
            pltpu.VMEM((low.shape[1], weights.shape[0]), BF16),
            pltpu.VMEM((group, back.shape[0]), BF16),
            pltpu.VMEM((group, low.shape[1]), BF16),
        ],
        compiler_params=pltpu.CompilerParams(vmem_limit_bytes=LIMIT),
        name="finish",
    )(full, labels, tall, low, rows, base, back, weights)


def exchange(block, axis):
    return lax.all_to_all(block, axis, split_axis=0, concat_axis=0, tiled=True)


SIDE = 4


def neighbour(block, dim, step):
    def to(i):
        at = [i // SIDE, i % SIDE]
        at[dim] = (at[dim] + step) % SIDE
        return at[0] * SIDE + at[1]

    return lax.ppermute(block, "adapter", [(i, to(i)) for i in range(SIDE * SIDE)])


def send_ring(block, dim):
    quarter = block.shape[0] // SIDE
    parts = [block[i * quarter : (i + 1) * quarter] for i in range(SIDE)]
    return [parts[0]] + [neighbour(parts[i], dim, i) for i in range(1, SIDE)]


def keep(got, away):
    return jnp.where(
        away == 0, got[0], jnp.where(away == 1, got[1], jnp.where(away == 2, got[2], got[3]))
    )


def scatter_start(matrix):
    half = matrix.shape[0] // 2
    return [send_ring(matrix[:half], 0), send_ring(matrix[half:], 1)]


def scatter_end(started, root):
    me = lax.axis_index("adapter").astype(I32)
    away = ((me // SIDE - root // SIDE) % SIDE, (me % SIDE - root % SIDE) % SIDE)
    parts = []
    for first, got in enumerate(started):
        second = 1 - first
        parts.append(keep(send_ring(keep(got, away[first]), second), away[second]))
    return jnp.concatenate(parts, axis=0)


def scattered_order(root, held):
    member, slot = jnp.arange(held) // 4, jnp.arange(held) % 4
    x, z = (member // SIDE - root // SIDE) % SIDE, (member % SIDE - root % SIDE) % SIDE
    quarter = held // 2 // SIDE
    sixteenth = quarter // SIDE
    one = x * quarter + z * sixteenth + slot
    other = held // 2 + z * quarter + x * sixteenth + slot - 2
    return jnp.where(slot < 2, one, other).astype(I32)


def swapped(block, bit):
    members = lax.axis_size("tensor")
    return lax.ppermute(block, "tensor", [(i, i ^ bit) for i in range(members)])


def total_over_tensor(part):
    part = part + swapped(part, 1)
    others = [swapped(part, bit) for bit in (2, 4, 6)]
    return (part + others[0]) + (others[1] + others[2])


def per_device(
    tokens, token_adapter_index, joined_weight_matrix, adapter_down_weight, adapter_up_weight
):
    owners = lax.axis_size("adapter")
    members = lax.axis_size("tensor")
    local_rows, width = tokens.shape
    group = members * local_rows
    held, rank, features = adapter_down_weight.shape
    columns = adapter_up_weight.shape[2]
    capacity = 4 * group // owners
    even = group // owners
    down = adapter_down_weight.reshape(held * rank, features)
    up = adapter_up_weight.reshape(held * rank, columns)
    wide = features + LANES

    order = jnp.arange(held, dtype=I32)
    gathered = lax.all_gather(tokens, "tensor", axis=0, tiled=True)
    started = scatter_start(jnp.concatenate([down, up], axis=1))
    ids = lax.all_gather(token_adapter_index, "tensor", axis=0, tiled=True)
    started, ids = lax.optimization_barrier((started, ids))
    info, tall = plan(ids, owners, held, even)

    named = info[3, 0]
    piece = scatter_end(started, named)
    weights = lax.all_gather(piece, "adapter", axis=0, tiled=True)
    labels = scattered_order(named, held)

    here = lax.axis_index("tensor").astype(I32).reshape(1)
    send, rest_rows = route(here, info, gathered, features, owners, even, capacity)
    rows = exchange(send.reshape(owners, even, wide), "adapter")

    said = rows[:, 0, features + 3 : features + 6].astype(I32)
    same = jnp.all(said[:, 0] == said[0, 0])
    full = jnp.where(same, said[0, 0], -1)
    largest = jnp.where(same, jnp.max(said[:, 1]), jnp.max(said[:, 2]))
    turns = (largest + even - 1) // even

    base = jnp.dot(gathered, joined_weight_matrix, preferred_element_type=F32)
    rows, base = lax.optimization_barrier((rows, base))

    rows = rows.reshape(owners * even, wide)
    part, _ = low_part(order, rows, down, rank, SMALL)
    low = total_over_tensor(part).astype(BF16)
    delta = delta_of(low, rows, up, 256)
    rest_rows, delta, full, turns, labels = lax.optimization_barrier(
        (rest_rows, delta, full, turns, labels)
    )
    back = exchange(delta.reshape(owners, even, columns), "adapter").reshape(owners * even, columns)

    owner, place = info[0], info[2]

    def more(carry):
        turn, total = carry
        turn, source = lax.optimization_barrier((turn, gathered))
        wanted = (owner != full) & (place // even == turn)
        slot = jnp.where(wanted, owner * even + place % even, -1)
        chosen = (slot[None, :] == jnp.arange(owners * even, dtype=I32)[:, None]).astype(BF16)
        mine = lax.dynamic_slice_in_dim(source, here[0] * features, features, 1)
        numbers = jnp.pad(info[1][:, None].astype(BF16), ((0, 0), (1, LANES - 2)))
        mine = jnp.concatenate([mine, numbers], axis=1)
        moved = jnp.dot(chosen, mine, preferred_element_type=F32).astype(BF16)
        moved = exchange(moved.reshape(owners, even, wide), "adapter").reshape(owners * even, wide)
        more_part, _ = low_part(order, moved, down, rank, SMALL)
        more_low = total_over_tensor(more_part).astype(BF16)
        more_delta = delta_of(more_low, moved, up, 256).reshape(owners, even, columns)
        more_back = exchange(more_delta, "adapter").reshape(owners * even, columns)
        return turn + 1, total + jnp.dot(chosen.T, more_back, preferred_element_type=F32)

    _, base = lax.while_loop(lambda carry: carry[0] < turns, more, (jnp.int32(1), base))

    rest_part, _ = low_part(labels, rest_rows, weights, rank, LIMIT)
    rest_low = total_over_tensor(rest_part).astype(BF16)
    places = jnp.broadcast_to(jnp.repeat(labels, rank)[None], (8, held * rank))
    return finish(full.reshape(1), places, tall, rest_low, rest_rows, base, back, weights, even, 256)


def solution(mesh):
    return jax.shard_map(
        per_device,
        mesh=mesh,
        in_specs=(
            P(("adapter", "tensor"), None),
            P(("adapter", "tensor")),
            P(None, "tensor"),
            P("adapter", None, "tensor"),
            P("adapter", None, "tensor"),
        ),
        out_specs=P("adapter", "tensor"),
        check_vma=False,
    )
```

```python
import functools

import jax
import jax.numpy as jnp
from jax import lax
from jax.experimental import pallas as pl
from jax.experimental.pallas import tpu as pltpu
from jax.sharding import PartitionSpec as P

BF16, F32, I32 = jnp.bfloat16, jnp.float32, jnp.int32
LANES = 128
VMEM = pl.BlockSpec(memory_space=pltpu.VMEM)
LIMIT = 24 * 1024 * 1024


def iota(shape, dim):
    return lax.broadcasted_iota(I32, shape, dim)


def rows_by_rows(a, b):
    return lax.dot_general(a, b, (((1,), (1,)), ((), ())), preferred_element_type=F32)


def columns_by_columns(a, b):
    return lax.dot_general(a, b, (((0,), (0,)), ((), ())), preferred_element_type=F32)


def lane_as_row(extra, lane):
    pick = (iota((8, LANES), 1) == lane).astype(BF16)
    return rows_by_rows(pick, extra).astype(I32)


def plan_kernel(owners, held, even, ids_ref, info_ref, down_ref):
    group = ids_ref.shape[1]
    ids = ids_ref[...]
    owner = ids // held
    hot = iota((owners, group), 0) == owner[0:1]
    earlier = (iota((group, group), 0) < iota((group, group), 1)).astype(BF16)
    before = jnp.dot(hot.astype(BF16), earlier, preferred_element_type=F32)
    place = jnp.sum(jnp.where(hot, before, 0.0), axis=0, keepdims=True).astype(I32)
    counts = jnp.sum(jnp.where(hot, 1, 0), axis=1, keepdims=True)
    most = jnp.max(counts, axis=0, keepdims=True)
    number = iota((owners, 1), 0)
    full = jnp.min(jnp.where(counts == most, number, owners), axis=0, keepdims=True)
    others = jnp.max(jnp.where(number == full, 0, counts), axis=0, keepdims=True)
    info = jnp.broadcast_to(most, (8, group))
    line = iota((8, group), 0)
    for i, value in enumerate((owner, ids - owner * held, place, full, others)):
        info = jnp.where(line == i, value, info)
    info_ref[...] = info
    tall = jnp.concatenate([info.astype(F32), jnp.zeros((LANES - 8, group), F32)], axis=0)
    down_ref[...] = tall.T.astype(I32)


def plan(ids, owners, held, even):
    return pl.pallas_call(
        functools.partial(plan_kernel, owners, held, even),
        out_shape=(
            jax.ShapeDtypeStruct((8, ids.shape[0]), I32),
            jax.ShapeDtypeStruct((ids.shape[0], LANES), I32),
        ),
        in_specs=[VMEM],
        out_specs=(VMEM, VMEM),
        compiler_params=pltpu.CompilerParams(vmem_limit_bytes=LIMIT),
        name="plan",
    )(jnp.broadcast_to(ids[None], (8, ids.shape[0])))


def route_kernel(owners, even, at_ref, info_ref, rows_ref, main_ref, rest_ref):
    group, features = rows_ref.shape
    slots, spare_slots = main_ref.shape[0], rest_ref.shape[0]
    info = info_ref[...]
    owner, local, place, full = info[0:1], info[1:2], info[2:3], info[3:4]
    rows = rows_ref[...]
    numbers = jnp.where(iota((LANES, group), 0) == 1, local, 0).astype(F32).astype(BF16)

    target = jnp.where(place < even, owner * even + place, -1)
    chosen = (iota((slots, group), 0) == target).astype(BF16)
    main_ref[:, :features] = jnp.dot(chosen, rows, preferred_element_type=F32).astype(BF16)
    tail = rows_by_rows(chosen, numbers)
    lane = iota(tail.shape, 1)
    for i in (3, 4, 5):
        tail = jnp.where(lane == i, info[i : i + 1, 0:1].astype(F32), tail)
    main_ref[:, features:] = tail.astype(BF16)

    spare = jnp.where((owner == full) & (place >= even), place - even, -1)
    chosen = (iota((spare_slots, group), 0) == spare).astype(BF16)
    rest_ref[:, :features] = jnp.dot(chosen, rows, preferred_element_type=F32).astype(BF16)
    rest_ref[:, features:] = rows_by_rows(chosen, numbers).astype(BF16)


def route(at, info, gathered, features, owners, even, spare_slots):
    group = gathered.shape[0]
    wide = features + LANES
    return pl.pallas_call(
        functools.partial(route_kernel, owners, even),
        grid_spec=pltpu.PrefetchScalarGridSpec(
            num_scalar_prefetch=1,
            grid=(1,),
            in_specs=[
                pl.BlockSpec((8, group), lambda i, at: (0, 0)),
                pl.BlockSpec((group, features), lambda i, at: (0, at[0])),
            ],
            out_specs=(
                pl.BlockSpec((owners * even, wide), lambda i, at: (0, 0)),
                pl.BlockSpec((spare_slots, wide), lambda i, at: (0, 0)),
            ),
        ),
        out_shape=(
            jax.ShapeDtypeStruct((owners * even, wide), BF16),
            jax.ShapeDtypeStruct((spare_slots, wide), BF16),
        ),
        compiler_params=pltpu.CompilerParams(vmem_limit_bytes=LIMIT),
        name="route",
    )(at, info, gathered)


def low_kernel(rank, labels_ref, rows_ref, down_ref, low_ref):
    features = rows_ref.shape[1] - LANES
    local = lane_as_row(rows_ref[:, features:], 1)
    wide = rows_by_rows(down_ref[:, :features], rows_ref[:, :features])
    total = jnp.zeros(low_ref.shape, F32)
    for i in range(down_ref.shape[0] // rank):
        total += jnp.where(local[0:1] == labels_ref[i], wide[i * rank : (i + 1) * rank], 0.0)
    low_ref[...] = total


def low_part(labels, rows, down, rank):
    count, wide = rows.shape
    return pl.pallas_call(
        functools.partial(low_kernel, rank),
        out_shape=jax.ShapeDtypeStruct((rank, count), F32),
        in_specs=[pl.BlockSpec(memory_space=pltpu.SMEM), VMEM, VMEM],
        out_specs=VMEM,
        compiler_params=pltpu.CompilerParams(vmem_limit_bytes=LIMIT),
        cost_estimate=pl.CostEstimate(
            flops=2 * count * down.shape[0] * wide,
            bytes_accessed=2 * wide * (count + down.shape[0]),
            transcendentals=0,
        ),
        name="low",
    )(labels, rows, down)


def spread(low, local, labels):
    rank, places = low.shape[0], labels.shape[1]
    repeat = (iota((rank, places), 1) % rank == iota((rank, places), 0)).astype(BF16)
    values = columns_by_columns(low, repeat)
    return jnp.where(local == labels, values, 0.0).astype(BF16)


def row_locals(rows_ref):
    lane = rows_ref.shape[1] - LANES + 1
    return rows_ref[:, lane : lane + 1].astype(F32).astype(I32)


def delta_kernel(low_ref, rows_ref, up_ref, out_ref):
    places = up_ref.shape[0]
    labels = iota((1, places), 1) // low_ref.shape[0]
    wide = spread(low_ref[...].astype(BF16), row_locals(rows_ref), labels)
    out_ref[...] = (2.0 * jnp.dot(wide, up_ref[...], preferred_element_type=F32)).astype(BF16)


def delta_of(low, rows, up):
    count, columns = rows.shape[0], up.shape[1]
    return pl.pallas_call(
        delta_kernel,
        out_shape=jax.ShapeDtypeStruct((count, columns), BF16),
        in_specs=[VMEM] * 3,
        out_specs=VMEM,
        compiler_params=pltpu.CompilerParams(vmem_limit_bytes=LIMIT),
        cost_estimate=pl.CostEstimate(
            flops=2 * count * up.size, bytes_accessed=2 * (up.size + count * columns), transcendentals=0
        ),
        name="delta",
    )(low, rows, up)


def add_kernel(even, tall_ref, base_ref, back_ref, out_ref):
    owner, place = tall_ref[:, 0:1], tall_ref[:, 2:3]
    target = jnp.where(place < even, owner * even + place, -1)
    chosen = (iota((tall_ref.shape[0], back_ref.shape[0]), 1) == target).astype(BF16)
    out_ref[...] = base_ref[...] + jnp.dot(chosen, back_ref[...], preferred_element_type=F32)


def add_back(tall, base, back, even):
    return pl.pallas_call(
        functools.partial(add_kernel, even),
        out_shape=jax.ShapeDtypeStruct(base.shape, F32),
        in_specs=[VMEM] * 3,
        out_specs=VMEM,
        compiler_params=pltpu.CompilerParams(vmem_limit_bytes=LIMIT),
        cost_estimate=pl.CostEstimate(
            flops=2 * back.size * base.shape[0], bytes_accessed=8 * base.size + 2 * back.size, transcendentals=0
        ),
        name="add_back",
    )(tall, base, back)


def finish_kernel(even, full_ref, labels_ref, tall_ref, low_ref, rows_ref, base_ref, weights_ref, out_ref):
    group, columns = base_ref.shape
    owner, place = tall_ref[:, 0:1], tall_ref[:, 2:3]
    spare = jnp.where((owner == full_ref[0]) & (place >= even), place - even, -1)
    chosen = (iota((group, rows_ref.shape[0]), 1) == spare).astype(BF16)
    wide = spread(low_ref[...].astype(BF16), row_locals(rows_ref), labels_ref[0:1])
    up = weights_ref[:, weights_ref.shape[1] - columns :]
    delta = (2.0 * jnp.dot(wide, up, preferred_element_type=F32)).astype(BF16)
    added = jnp.dot(chosen, delta, preferred_element_type=F32)
    out_ref[...] = (base_ref[...] + added).astype(BF16)


def finish(full, labels, tall, low, rows, base, weights, even):
    return pl.pallas_call(
        functools.partial(finish_kernel, even),
        out_shape=jax.ShapeDtypeStruct(base.shape, BF16),
        in_specs=[pl.BlockSpec(memory_space=pltpu.SMEM)] + [VMEM] * 6,
        out_specs=VMEM,
        compiler_params=pltpu.CompilerParams(vmem_limit_bytes=LIMIT),
        cost_estimate=pl.CostEstimate(
            flops=4 * weights.size * rows.shape[0], bytes_accessed=6 * base.size, transcendentals=0
        ),
        name="finish",
    )(full, labels, tall, low, rows, base, weights)


def exchange(block, axis):
    return lax.all_to_all(block, axis, split_axis=0, concat_axis=0, tiled=True)


SIDE = 4


def neighbour(block, dim, step):
    def to(i):
        at = [i // SIDE, i % SIDE]
        at[dim] = (at[dim] + step) % SIDE
        return at[0] * SIDE + at[1]

    return lax.ppermute(block, "adapter", [(i, to(i)) for i in range(SIDE * SIDE)])


def send_ring(block, dim):
    quarter = block.shape[0] // SIDE
    parts = [block[i * quarter : (i + 1) * quarter] for i in range(SIDE)]
    return [parts[0]] + [neighbour(parts[i], dim, i) for i in range(1, SIDE)]


def keep(got, away):
    return jnp.where(
        away == 0, got[0], jnp.where(away == 1, got[1], jnp.where(away == 2, got[2], got[3]))
    )


def scatter_start(matrix):
    half = matrix.shape[0] // 2
    return [send_ring(matrix[:half], 0), send_ring(matrix[half:], 1)]


def away_from(root):
    me = lax.axis_index("adapter").astype(I32)
    return (me // SIDE - root // SIDE) % SIDE, (me % SIDE - root % SIDE) % SIDE


def scatter_end(started, away):
    parts = []
    for first, got in enumerate(started):
        second = 1 - first
        parts.append(keep(send_ring(keep(got, away[first]), second), away[second]))
    return jnp.concatenate(parts, axis=0)


def scattered_order(root, held):
    member, slot = jnp.arange(held) // 4, jnp.arange(held) % 4
    x, z = (member // SIDE - root // SIDE) % SIDE, (member % SIDE - root % SIDE) % SIDE
    quarter = held // 2 // SIDE
    sixteenth = quarter // SIDE
    one = x * quarter + z * sixteenth + slot
    other = held // 2 + z * quarter + x * sixteenth + slot - 2
    return jnp.where(slot < 2, one, other).astype(I32)


def swapped(block, bit):
    members = lax.axis_size("tensor")
    return lax.ppermute(block, "tensor", [(i, i ^ bit) for i in range(members)])


def total_over_tensor(part, beside=None):
    part = part + swapped(part, 1)
    others = [swapped(part, bit) for bit in (2, 4, 6)]
    others, beside = lax.optimization_barrier((others, beside))
    return (part + others[0]) + (others[1] + others[2]), beside


def per_device(
    tokens, token_adapter_index, joined_weight_matrix, adapter_down_weight, adapter_up_weight
):
    owners = lax.axis_size("adapter")
    members = lax.axis_size("tensor")
    local_rows, width = tokens.shape
    group = members * local_rows
    held, rank, features = adapter_down_weight.shape
    columns = adapter_up_weight.shape[2]
    capacity = 4 * group // owners
    even = group // owners
    down = adapter_down_weight.reshape(held * rank, features)
    up = adapter_up_weight.reshape(held * rank, columns)
    wide = features + LANES

    order = jnp.arange(held, dtype=I32)
    started = scatter_start(jnp.concatenate([down, up], axis=1))

    gathered = lax.all_gather(tokens, "tensor", axis=0, tiled=True)
    ids = lax.all_gather(token_adapter_index, "tensor", axis=0, tiled=True)
    info, tall = plan(ids, owners, held, even)

    named = info[3, 0]
    started, away = lax.optimization_barrier((started, away_from(named)))
    piece = scatter_end(started, away)
    weights = lax.all_gather(piece, "adapter", axis=0, tiled=True)
    labels = scattered_order(named, held)

    here = lax.axis_index("tensor").astype(I32).reshape(1)
    send, rest_rows = route(here, info, gathered, features, owners, even, capacity)
    rows = exchange(send.reshape(owners, even, wide), "adapter")

    said = rows[:, 0, features + 3 : features + 6].astype(I32)
    same = jnp.all(said[:, 0] == said[0, 0])
    full = jnp.where(same, said[0, 0], -1)
    largest = jnp.where(same, jnp.max(said[:, 1]), jnp.max(said[:, 2]))
    turns = (largest + even - 1) // even

    base = jnp.dot(gathered, joined_weight_matrix, preferred_element_type=F32)
    rows, base = lax.optimization_barrier((rows, base))

    rows = rows.reshape(owners * even, wide)
    low, _ = total_over_tensor(low_part(order, rows, down, rank))
    delta = delta_of(low, rows, up)
    places = jnp.broadcast_to(jnp.repeat(labels, rank)[None], (8, held * rank))
    rest_rows, delta, full, turns, labels, places = lax.optimization_barrier(
        (rest_rows, delta, full, turns, labels, places)
    )
    back = exchange(delta.reshape(owners, even, columns), "adapter").reshape(owners * even, columns)

    owner, place = info[0], info[2]

    def more(carry):
        turn, total = carry
        turn, source = lax.optimization_barrier((turn, gathered))
        wanted = (owner != full) & (place // even == turn)
        slot = jnp.where(wanted, owner * even + place % even, -1)
        chosen = (slot[None, :] == jnp.arange(owners * even, dtype=I32)[:, None]).astype(BF16)
        mine = lax.dynamic_slice_in_dim(source, here[0] * features, features, 1)
        numbers = jnp.pad(info[1][:, None].astype(BF16), ((0, 0), (1, LANES - 2)))
        mine = jnp.concatenate([mine, numbers], axis=1)
        moved = jnp.dot(chosen, mine, preferred_element_type=F32).astype(BF16)
        moved = exchange(moved.reshape(owners, even, wide), "adapter").reshape(owners * even, wide)
        more_low, _ = total_over_tensor(low_part(order, moved, down, rank))
        more_delta = delta_of(more_low, moved, up).reshape(owners, even, columns)
        more_back = exchange(more_delta, "adapter").reshape(owners * even, columns)
        return turn + 1, total + jnp.dot(chosen.T, more_back, preferred_element_type=F32)

    _, base = lax.while_loop(lambda carry: carry[0] < turns, more, (jnp.int32(1), base))

    base = add_back(tall, base, back, even)

    rest_low, base = total_over_tensor(low_part(labels, rest_rows, weights, rank), base)
    return finish(full.reshape(1), places, tall, rest_low, rest_rows, base, weights, even)


def solution(mesh):
    return jax.shard_map(
        per_device,
        mesh=mesh,
        in_specs=(
            P(("adapter", "tensor"), None),
            P(("adapter", "tensor")),
            P(None, "tensor"),
            P("adapter", None, "tensor"),
            P("adapter", None, "tensor"),
        ),
        out_specs=P("adapter", "tensor"),
        check_vma=False,
    )
```

```python
import functools

import jax
import jax.numpy as jnp
from jax import lax
from jax.experimental import pallas as pl
from jax.experimental.pallas import tpu as pltpu
from jax.sharding import PartitionSpec as P

BF16, F32, I32 = jnp.bfloat16, jnp.float32, jnp.int32
LANES = 128
VMEM = pl.BlockSpec(memory_space=pltpu.VMEM)
LIMIT = 24 * 1024 * 1024


def iota(shape, dim):
    return lax.broadcasted_iota(I32, shape, dim)


def rows_by_rows(a, b):
    return lax.dot_general(a, b, (((1,), (1,)), ((), ())), preferred_element_type=F32)


def columns_by_columns(a, b):
    return lax.dot_general(a, b, (((0,), (0,)), ((), ())), preferred_element_type=F32)


def lane_as_row(extra, lane):
    pick = (iota((8, LANES), 1) == lane).astype(BF16)
    return rows_by_rows(pick, extra).astype(I32)


def plan_kernel(owners, held, even, ids_ref, info_ref, down_ref):
    group = ids_ref.shape[1]
    ids = ids_ref[...]
    owner = ids // held
    hot = iota((owners, group), 0) == owner[0:1]
    earlier = (iota((group, group), 0) < iota((group, group), 1)).astype(BF16)
    before = jnp.dot(hot.astype(BF16), earlier, preferred_element_type=F32)
    place = jnp.sum(jnp.where(hot, before, 0.0), axis=0, keepdims=True).astype(I32)
    counts = jnp.sum(jnp.where(hot, 1, 0), axis=1, keepdims=True)
    most = jnp.max(counts, axis=0, keepdims=True)
    number = iota((owners, 1), 0)
    full = jnp.min(jnp.where(counts == most, number, owners), axis=0, keepdims=True)
    others = jnp.max(jnp.where(number == full, 0, counts), axis=0, keepdims=True)
    info = jnp.broadcast_to(most, (8, group))
    line = iota((8, group), 0)
    for i, value in enumerate((owner, ids - owner * held, place, full, others)):
        info = jnp.where(line == i, value, info)
    info_ref[...] = info
    tall = jnp.concatenate([info.astype(F32), jnp.zeros((LANES - 8, group), F32)], axis=0)
    down_ref[...] = tall.T.astype(I32)


def plan(ids, owners, held, even):
    return pl.pallas_call(
        functools.partial(plan_kernel, owners, held, even),
        out_shape=(
            jax.ShapeDtypeStruct((8, ids.shape[0]), I32),
            jax.ShapeDtypeStruct((ids.shape[0], LANES), I32),
        ),
        in_specs=[VMEM],
        out_specs=(VMEM, VMEM),
        compiler_params=pltpu.CompilerParams(vmem_limit_bytes=LIMIT),
        name="plan",
    )(jnp.broadcast_to(ids[None], (8, ids.shape[0])))


def route_kernel(owners, even, at_ref, info_ref, rows_ref, main_ref, rest_ref):
    group, features = rows_ref.shape
    slots, spare_slots = main_ref.shape[0], rest_ref.shape[0]
    info = info_ref[...]
    owner, local, place, full = info[0:1], info[1:2], info[2:3], info[3:4]
    rows = rows_ref[...]
    numbers = jnp.where(iota((LANES, group), 0) == 1, local, 0).astype(F32).astype(BF16)

    target = jnp.where(place < even, owner * even + place, -1)
    chosen = (iota((slots, group), 0) == target).astype(BF16)
    main_ref[:, :features] = jnp.dot(chosen, rows, preferred_element_type=F32).astype(BF16)
    tail = rows_by_rows(chosen, numbers)
    lane = iota(tail.shape, 1)
    for i in (3, 4, 5):
        tail = jnp.where(lane == i, info[i : i + 1, 0:1].astype(F32), tail)
    main_ref[:, features:] = tail.astype(BF16)

    spare = jnp.where((owner == full) & (place >= even), place - even, -1)
    chosen = (iota((spare_slots, group), 0) == spare).astype(BF16)
    rest_ref[:, :features] = jnp.dot(chosen, rows, preferred_element_type=F32).astype(BF16)
    rest_ref[:, features:] = rows_by_rows(chosen, numbers).astype(BF16)


def route(at, info, gathered, features, owners, even, spare_slots):
    group = gathered.shape[0]
    wide = features + LANES
    return pl.pallas_call(
        functools.partial(route_kernel, owners, even),
        grid_spec=pltpu.PrefetchScalarGridSpec(
            num_scalar_prefetch=1,
            grid=(1,),
            in_specs=[
                pl.BlockSpec((8, group), lambda i, at: (0, 0)),
                pl.BlockSpec((group, features), lambda i, at: (0, at[0])),
            ],
            out_specs=(
                pl.BlockSpec((owners * even, wide), lambda i, at: (0, 0)),
                pl.BlockSpec((spare_slots, wide), lambda i, at: (0, 0)),
            ),
        ),
        out_shape=(
            jax.ShapeDtypeStruct((owners * even, wide), BF16),
            jax.ShapeDtypeStruct((spare_slots, wide), BF16),
        ),
        compiler_params=pltpu.CompilerParams(vmem_limit_bytes=LIMIT),
        name="route",
    )(at, info, gathered)


def low_kernel(rank, labels_ref, rows_ref, down_ref, low_ref):
    features = rows_ref.shape[1] - LANES
    local = lane_as_row(rows_ref[:, features:], 1)
    wide = rows_by_rows(down_ref[:, :features], rows_ref[:, :features])
    total = jnp.zeros(low_ref.shape, F32)
    for i in range(down_ref.shape[0] // rank):
        total += jnp.where(local[0:1] == labels_ref[i], wide[i * rank : (i + 1) * rank], 0.0)
    low_ref[...] = total


def low_part(labels, rows, down, rank):
    count, wide = rows.shape
    return pl.pallas_call(
        functools.partial(low_kernel, rank),
        out_shape=jax.ShapeDtypeStruct((rank, count), F32),
        in_specs=[pl.BlockSpec(memory_space=pltpu.SMEM), VMEM, VMEM],
        out_specs=VMEM,
        compiler_params=pltpu.CompilerParams(vmem_limit_bytes=LIMIT),
        cost_estimate=pl.CostEstimate(
            flops=2 * count * down.shape[0] * wide,
            bytes_accessed=2 * wide * (count + down.shape[0]),
            transcendentals=0,
        ),
        name="low",
    )(labels, rows, down)


def spread(low, local, labels):
    rank, places = low.shape[0], labels.shape[1]
    repeat = (iota((rank, places), 1) % rank == iota((rank, places), 0)).astype(BF16)
    values = columns_by_columns(low, repeat)
    return jnp.where(local == labels, values, 0.0).astype(BF16)


def row_locals(rows_ref):
    lane = rows_ref.shape[1] - LANES + 1
    return rows_ref[:, lane : lane + 1].astype(F32).astype(I32)


def delta_kernel(low_ref, rows_ref, up_ref, out_ref):
    places = up_ref.shape[0]
    labels = iota((1, places), 1) // low_ref.shape[0]
    wide = spread(low_ref[...].astype(BF16), row_locals(rows_ref), labels)
    out_ref[...] = (2.0 * jnp.dot(wide, up_ref[...], preferred_element_type=F32)).astype(BF16)


def delta_of(low, rows, up):
    count, columns = rows.shape[0], up.shape[1]
    return pl.pallas_call(
        delta_kernel,
        out_shape=jax.ShapeDtypeStruct((count, columns), BF16),
        in_specs=[VMEM] * 3,
        out_specs=VMEM,
        compiler_params=pltpu.CompilerParams(vmem_limit_bytes=LIMIT),
        cost_estimate=pl.CostEstimate(
            flops=2 * count * up.size, bytes_accessed=2 * (up.size + count * columns), transcendentals=0
        ),
        name="delta",
    )(low, rows, up)


def add_kernel(even, tall_ref, base_ref, back_ref, out_ref):
    owner, place = tall_ref[:, 0:1], tall_ref[:, 2:3]
    target = jnp.where(place < even, owner * even + place, -1)
    chosen = (iota((tall_ref.shape[0], back_ref.shape[0]), 1) == target).astype(BF16)
    out_ref[...] = base_ref[...] + jnp.dot(chosen, back_ref[...], preferred_element_type=F32)


def add_back(tall, base, back, even):
    return pl.pallas_call(
        functools.partial(add_kernel, even),
        out_shape=jax.ShapeDtypeStruct(base.shape, F32),
        in_specs=[VMEM] * 3,
        out_specs=VMEM,
        compiler_params=pltpu.CompilerParams(vmem_limit_bytes=LIMIT),
        cost_estimate=pl.CostEstimate(
            flops=2 * back.size * base.shape[0], bytes_accessed=8 * base.size + 2 * back.size, transcendentals=0
        ),
        name="add_back",
    )(tall, base, back)


def finish_kernel(even, full_ref, labels_ref, tall_ref, low_ref, rows_ref, base_ref, weights_ref, out_ref):
    group, columns = base_ref.shape
    owner, place = tall_ref[:, 0:1], tall_ref[:, 2:3]
    spare = jnp.where((owner == full_ref[0]) & (place >= even), place - even, -1)
    chosen = (iota((group, rows_ref.shape[0]), 1) == spare).astype(BF16)
    wide = spread(low_ref[...].astype(BF16), row_locals(rows_ref), labels_ref[0:1])
    up = weights_ref[:, weights_ref.shape[1] - columns :]
    delta = (2.0 * jnp.dot(wide, up, preferred_element_type=F32)).astype(BF16)
    added = jnp.dot(chosen, delta, preferred_element_type=F32)
    out_ref[...] = (base_ref[...] + added).astype(BF16)


def finish(full, labels, tall, low, rows, base, weights, even):
    return pl.pallas_call(
        functools.partial(finish_kernel, even),
        out_shape=jax.ShapeDtypeStruct(base.shape, BF16),
        in_specs=[pl.BlockSpec(memory_space=pltpu.SMEM)] + [VMEM] * 6,
        out_specs=VMEM,
        compiler_params=pltpu.CompilerParams(vmem_limit_bytes=LIMIT),
        cost_estimate=pl.CostEstimate(
            flops=4 * weights.size * rows.shape[0], bytes_accessed=6 * base.size, transcendentals=0
        ),
        name="finish",
    )(full, labels, tall, low, rows, base, weights)


def exchange(block, axis):
    return lax.all_to_all(block, axis, split_axis=0, concat_axis=0, tiled=True)


SIDE = 4


def neighbour(block, dim, step):
    def to(i):
        at = [i // SIDE, i % SIDE]
        at[dim] = (at[dim] + step) % SIDE
        return at[0] * SIDE + at[1]

    return lax.ppermute(block, "adapter", [(i, to(i)) for i in range(SIDE * SIDE)])


def send_ring(block, dim):
    quarter = block.shape[0] // SIDE
    parts = [block[i * quarter : (i + 1) * quarter] for i in range(SIDE)]
    return [parts[0]] + [neighbour(parts[i], dim, i) for i in range(1, SIDE)]


def keep(got, away):
    return jnp.where(
        away == 0, got[0], jnp.where(away == 1, got[1], jnp.where(away == 2, got[2], got[3]))
    )


def scatter_start(matrix):
    half = matrix.shape[0] // 2
    return [send_ring(matrix[:half], 0), send_ring(matrix[half:], 1)]


def away_from(root):
    me = lax.axis_index("adapter").astype(I32)
    return (me // SIDE - root // SIDE) % SIDE, (me % SIDE - root % SIDE) % SIDE


def scatter_end(started, away):
    parts = []
    for first, got in enumerate(started):
        second = 1 - first
        parts.append(keep(send_ring(keep(got, away[first]), second), away[second]))
    return jnp.concatenate(parts, axis=0)


def scattered_order(root, held):
    member, slot = jnp.arange(held) // 4, jnp.arange(held) % 4
    x, z = (member // SIDE - root // SIDE) % SIDE, (member % SIDE - root % SIDE) % SIDE
    quarter = held // 2 // SIDE
    sixteenth = quarter // SIDE
    one = x * quarter + z * sixteenth + slot
    other = held // 2 + z * quarter + x * sixteenth + slot - 2
    return jnp.where(slot < 2, one, other).astype(I32)


def swapped(block, bit):
    members = lax.axis_size("tensor")
    return lax.ppermute(block, "tensor", [(i, i ^ bit) for i in range(members)])


def total_over_tensor(part, beside=None):
    part = part + swapped(part, 1)
    others = [swapped(part, bit) for bit in (2, 4, 6)]
    others, beside = lax.optimization_barrier((others, beside))
    return (part + others[0]) + (others[1] + others[2]), beside


def per_device(
    tokens, token_adapter_index, joined_weight_matrix, adapter_down_weight, adapter_up_weight
):
    owners = lax.axis_size("adapter")
    members = lax.axis_size("tensor")
    local_rows, width = tokens.shape
    group = members * local_rows
    held, rank, features = adapter_down_weight.shape
    columns = adapter_up_weight.shape[2]
    capacity = 4 * group // owners
    even = group // owners
    down = adapter_down_weight.reshape(held * rank, features)
    up = adapter_up_weight.reshape(held * rank, columns)
    wide = features + LANES

    order = jnp.arange(held, dtype=I32)
    started = scatter_start(jnp.concatenate([down, up], axis=1))

    gathered = lax.all_gather(tokens, "tensor", axis=0, tiled=True)
    ids = lax.all_gather(token_adapter_index, "tensor", axis=0, tiled=True)
    info, tall = plan(ids, owners, held, even)

    named = info[3, 0]
    started, away = lax.optimization_barrier((started, away_from(named)))
    piece = scatter_end(started, away)
    weights = lax.all_gather(piece, "adapter", axis=0, tiled=True)
    labels = scattered_order(named, held)

    here = lax.axis_index("tensor").astype(I32).reshape(1)
    send, rest_rows = route(here, info, gathered, features, owners, even, capacity)
    rows = exchange(send.reshape(owners, even, wide), "adapter")

    base = jnp.dot(gathered, joined_weight_matrix, preferred_element_type=F32)
    rows, base = lax.optimization_barrier((rows, base))

    rows = rows.reshape(owners * even, wide)
    low, _ = total_over_tensor(low_part(order, rows, down, rank))
    delta = delta_of(low, rows, up)
    places = jnp.broadcast_to(jnp.repeat(labels, rank)[None], (8, held * rank))
    said = rows.reshape(owners, even, wide)[:, 0, features + 3 : features + 6]
    rest_rows, delta, said, labels, places = lax.optimization_barrier(
        (rest_rows, delta, said, labels, places)
    )
    back = exchange(delta.reshape(owners, even, columns), "adapter").reshape(owners * even, columns)

    said = said.astype(I32)
    same = jnp.all(said[:, 0] == said[0, 0])
    full = jnp.where(same, said[0, 0], -1)
    largest = jnp.where(same, jnp.max(said[:, 1]), jnp.max(said[:, 2]))
    turns = (largest + even - 1) // even

    owner, place = info[0], info[2]

    def more(carry):
        turn, total = carry
        turn, source = lax.optimization_barrier((turn, gathered))
        wanted = (owner != full) & (place // even == turn)
        slot = jnp.where(wanted, owner * even + place % even, -1)
        chosen = (slot[None, :] == jnp.arange(owners * even, dtype=I32)[:, None]).astype(BF16)
        mine = lax.dynamic_slice_in_dim(source, here[0] * features, features, 1)
        numbers = jnp.pad(info[1][:, None].astype(BF16), ((0, 0), (1, LANES - 2)))
        mine = jnp.concatenate([mine, numbers], axis=1)
        moved = jnp.dot(chosen, mine, preferred_element_type=F32).astype(BF16)
        moved = exchange(moved.reshape(owners, even, wide), "adapter").reshape(owners * even, wide)
        more_low, _ = total_over_tensor(low_part(order, moved, down, rank))
        more_delta = delta_of(more_low, moved, up).reshape(owners, even, columns)
        more_back = exchange(more_delta, "adapter").reshape(owners * even, columns)
        return turn + 1, total + jnp.dot(chosen.T, more_back, preferred_element_type=F32)

    _, base = lax.while_loop(lambda carry: carry[0] < turns, more, (jnp.int32(1), base))

    base = add_back(tall, base, back, even)

    rest_low, base = total_over_tensor(low_part(labels, rest_rows, weights, rank), base)
    return finish(full.reshape(1), places, tall, rest_low, rest_rows, base, weights, even)


def solution(mesh):
    return jax.shard_map(
        per_device,
        mesh=mesh,
        in_specs=(
            P(("adapter", "tensor"), None),
            P(("adapter", "tensor")),
            P(None, "tensor"),
            P("adapter", None, "tensor"),
            P("adapter", None, "tensor"),
        ),
        out_specs=P("adapter", "tensor"),
        check_vma=False,
    )
```

```python
import functools

import jax
import jax.numpy as jnp
from jax import lax
from jax.experimental import pallas as pl
from jax.experimental.pallas import tpu as pltpu
from jax.sharding import PartitionSpec as P

BF16, F32, I32 = jnp.bfloat16, jnp.float32, jnp.int32
LANES = 128
VMEM = pl.BlockSpec(memory_space=pltpu.VMEM)
LIMIT = 24 * 1024 * 1024


def iota(shape, dim):
    return lax.broadcasted_iota(I32, shape, dim)


def rows_by_rows(a, b):
    return lax.dot_general(a, b, (((1,), (1,)), ((), ())), preferred_element_type=F32)


def columns_by_columns(a, b):
    return lax.dot_general(a, b, (((0,), (0,)), ((), ())), preferred_element_type=F32)


def lane_as_row(extra, lane):
    pick = (iota((8, LANES), 1) == lane).astype(BF16)
    return rows_by_rows(pick, extra).astype(I32)


def plan_kernel(owners, held, even, ids_ref, info_ref, down_ref):
    group = ids_ref.shape[1]
    ids = ids_ref[...]
    owner = ids // held
    hot = iota((owners, group), 0) == owner[0:1]
    earlier = (iota((group, group), 0) < iota((group, group), 1)).astype(BF16)
    before = jnp.dot(hot.astype(BF16), earlier, preferred_element_type=F32)
    place = jnp.sum(jnp.where(hot, before, 0.0), axis=0, keepdims=True).astype(I32)
    counts = jnp.sum(jnp.where(hot, 1, 0), axis=1, keepdims=True)
    most = jnp.max(counts, axis=0, keepdims=True)
    number = iota((owners, 1), 0)
    full = jnp.min(jnp.where(counts == most, number, owners), axis=0, keepdims=True)
    others = jnp.max(jnp.where(number == full, 0, counts), axis=0, keepdims=True)
    info = jnp.broadcast_to(most, (8, group))
    line = iota((8, group), 0)
    for i, value in enumerate((owner, ids - owner * held, place, full, others)):
        info = jnp.where(line == i, value, info)
    info_ref[...] = info
    tall = jnp.concatenate([info.astype(F32), jnp.zeros((LANES - 8, group), F32)], axis=0)
    down_ref[...] = tall.T.astype(I32)


def plan(ids, owners, held, even):
    return pl.pallas_call(
        functools.partial(plan_kernel, owners, held, even),
        out_shape=(
            jax.ShapeDtypeStruct((8, ids.shape[0]), I32),
            jax.ShapeDtypeStruct((ids.shape[0], LANES), I32),
        ),
        in_specs=[VMEM],
        out_specs=(VMEM, VMEM),
        compiler_params=pltpu.CompilerParams(vmem_limit_bytes=LIMIT),
        name="plan",
    )(jnp.broadcast_to(ids[None], (8, ids.shape[0])))


def route_kernel(owners, even, at_ref, info_ref, rows_ref, main_ref, rest_ref):
    group, features = rows_ref.shape
    slots, spare_slots = main_ref.shape[0], rest_ref.shape[0]
    info = info_ref[...]
    owner, local, place, full = info[0:1], info[1:2], info[2:3], info[3:4]
    rows = rows_ref[...]
    numbers = jnp.where(iota((LANES, group), 0) == 1, local, 0).astype(F32).astype(BF16)

    target = jnp.where(place < even, owner * even + place, -1)
    chosen = (iota((slots, group), 0) == target).astype(BF16)
    main_ref[:, :features] = jnp.dot(chosen, rows, preferred_element_type=F32).astype(BF16)
    tail = rows_by_rows(chosen, numbers)
    lane = iota(tail.shape, 1)
    for i in (3, 4, 5):
        tail = jnp.where(lane == i, info[i : i + 1, 0:1].astype(F32), tail)
    main_ref[:, features:] = tail.astype(BF16)

    spare = jnp.where((owner == full) & (place >= even), place - even, -1)
    chosen = (iota((spare_slots, group), 0) == spare).astype(BF16)
    rest_ref[:, :features] = jnp.dot(chosen, rows, preferred_element_type=F32).astype(BF16)
    rest_ref[:, features:] = rows_by_rows(chosen, numbers).astype(BF16)


def route(at, info, gathered, features, owners, even, spare_slots):
    group = gathered.shape[0]
    wide = features + LANES
    return pl.pallas_call(
        functools.partial(route_kernel, owners, even),
        grid_spec=pltpu.PrefetchScalarGridSpec(
            num_scalar_prefetch=1,
            grid=(1,),
            in_specs=[
                pl.BlockSpec((8, group), lambda i, at: (0, 0)),
                pl.BlockSpec((group, features), lambda i, at: (0, at[0])),
            ],
            out_specs=(
                pl.BlockSpec((owners * even, wide), lambda i, at: (0, 0)),
                pl.BlockSpec((spare_slots, wide), lambda i, at: (0, 0)),
            ),
        ),
        out_shape=(
            jax.ShapeDtypeStruct((owners * even, wide), BF16),
            jax.ShapeDtypeStruct((spare_slots, wide), BF16),
        ),
        compiler_params=pltpu.CompilerParams(vmem_limit_bytes=LIMIT),
        name="route",
    )(at, info, gathered)


def low_kernel(rank, labels_ref, rows_ref, down_ref, low_ref):
    features = rows_ref.shape[1] - LANES
    local = lane_as_row(rows_ref[:, features:], 1)
    wide = rows_by_rows(down_ref[:, :features], rows_ref[:, :features])
    total = jnp.zeros(low_ref.shape, F32)
    for i in range(down_ref.shape[0] // rank):
        total += jnp.where(local[0:1] == labels_ref[i], wide[i * rank : (i + 1) * rank], 0.0)
    low_ref[...] = total


def low_part(labels, rows, down, rank):
    count, wide = rows.shape
    return pl.pallas_call(
        functools.partial(low_kernel, rank),
        out_shape=jax.ShapeDtypeStruct((rank, count), F32),
        in_specs=[pl.BlockSpec(memory_space=pltpu.SMEM), VMEM, VMEM],
        out_specs=VMEM,
        compiler_params=pltpu.CompilerParams(vmem_limit_bytes=LIMIT),
        cost_estimate=pl.CostEstimate(
            flops=2 * count * down.shape[0] * wide,
            bytes_accessed=2 * wide * (count + down.shape[0]),
            transcendentals=0,
        ),
        name="low",
    )(labels, rows, down)


def spread(low, local, labels):
    rank, places = low.shape[0], labels.shape[1]
    repeat = (iota((rank, places), 1) % rank == iota((rank, places), 0)).astype(BF16)
    values = columns_by_columns(low, repeat)
    return jnp.where(local == labels, values, 0.0).astype(BF16)


def row_locals(rows_ref):
    lane = rows_ref.shape[1] - LANES + 1
    return rows_ref[:, lane : lane + 1].astype(F32).astype(I32)


def delta_kernel(low_ref, rows_ref, up_ref, out_ref):
    places = up_ref.shape[0]
    labels = iota((1, places), 1) // low_ref.shape[0]
    wide = spread(low_ref[...].astype(BF16), row_locals(rows_ref), labels)
    out_ref[...] = (2.0 * jnp.dot(wide, up_ref[...], preferred_element_type=F32)).astype(BF16)


def delta_of(low, rows, up):
    count, columns = rows.shape[0], up.shape[1]
    return pl.pallas_call(
        delta_kernel,
        out_shape=jax.ShapeDtypeStruct((count, columns), BF16),
        in_specs=[VMEM] * 3,
        out_specs=VMEM,
        compiler_params=pltpu.CompilerParams(vmem_limit_bytes=LIMIT),
        cost_estimate=pl.CostEstimate(
            flops=2 * count * up.size, bytes_accessed=2 * (up.size + count * columns), transcendentals=0
        ),
        name="delta",
    )(low, rows, up)


def finish_kernel(
    even, full_ref, labels_ref, tall_ref, low_ref, rows_ref, base_ref, back_ref, weights_ref, out_ref
):
    group, columns = base_ref.shape
    owner, place = tall_ref[:, 0:1], tall_ref[:, 2:3]
    spare = jnp.where((owner == full_ref[0]) & (place >= even), place - even, -1)
    chosen = (iota((group, rows_ref.shape[0]), 1) == spare).astype(BF16)
    wide = spread(low_ref[...].astype(BF16), row_locals(rows_ref), labels_ref[0:1])
    up = weights_ref[:, weights_ref.shape[1] - columns :]
    delta = (2.0 * jnp.dot(wide, up, preferred_element_type=F32)).astype(BF16)
    added = jnp.dot(chosen, delta, preferred_element_type=F32)
    target = jnp.where(place < even, owner * even + place, -1)
    main = (iota((group, back_ref.shape[0]), 1) == target).astype(BF16)
    added += jnp.dot(main, back_ref[...], preferred_element_type=F32)
    out_ref[...] = (base_ref[...] + added).astype(BF16)


def finish(full, labels, tall, low, rows, base, back, weights, even):
    return pl.pallas_call(
        functools.partial(finish_kernel, even),
        out_shape=jax.ShapeDtypeStruct(base.shape, BF16),
        in_specs=[pl.BlockSpec(memory_space=pltpu.SMEM)] + [VMEM] * 7,
        out_specs=VMEM,
        compiler_params=pltpu.CompilerParams(vmem_limit_bytes=LIMIT),
        cost_estimate=pl.CostEstimate(
            flops=4 * weights.size * rows.shape[0], bytes_accessed=6 * base.size, transcendentals=0
        ),
        name="finish",
    )(full, labels, tall, low, rows, base, back, weights)


def exchange(block, axis):
    return lax.all_to_all(block, axis, split_axis=0, concat_axis=0, tiled=True)


SIDE = 4


def neighbour(block, dim, step):
    def to(i):
        at = [i // SIDE, i % SIDE]
        at[dim] = (at[dim] + step) % SIDE
        return at[0] * SIDE + at[1]

    return lax.ppermute(block, "adapter", [(i, to(i)) for i in range(SIDE * SIDE)])


def send_ring(block, dim):
    quarter = block.shape[0] // SIDE
    parts = [block[i * quarter : (i + 1) * quarter] for i in range(SIDE)]
    return [parts[0]] + [neighbour(parts[i], dim, i) for i in range(1, SIDE)]


def keep(got, away):
    return jnp.where(
        away == 0, got[0], jnp.where(away == 1, got[1], jnp.where(away == 2, got[2], got[3]))
    )


def scatter_start(matrix):
    half = matrix.shape[0] // 2
    return [send_ring(matrix[:half], 0), send_ring(matrix[half:], 1)]


def away_from(root):
    me = lax.axis_index("adapter").astype(I32)
    return (me // SIDE - root // SIDE) % SIDE, (me % SIDE - root % SIDE) % SIDE


def scatter_end(started, away):
    parts = []
    for first, got in enumerate(started):
        second = 1 - first
        parts.append(keep(send_ring(keep(got, away[first]), second), away[second]))
    return jnp.concatenate(parts, axis=0)


def scattered_order(root, held):
    member, slot = jnp.arange(held) // 4, jnp.arange(held) % 4
    x, z = (member // SIDE - root // SIDE) % SIDE, (member % SIDE - root % SIDE) % SIDE
    quarter = held // 2 // SIDE
    sixteenth = quarter // SIDE
    one = x * quarter + z * sixteenth + slot
    other = held // 2 + z * quarter + x * sixteenth + slot - 2
    return jnp.where(slot < 2, one, other).astype(I32)


def swapped(block, bit):
    members = lax.axis_size("tensor")
    return lax.ppermute(block, "tensor", [(i, i ^ bit) for i in range(members)])


def total_over_tensor(part, beside=None):
    part = part + swapped(part, 1)
    others = [swapped(part, bit) for bit in (2, 4, 6)]
    others, beside = lax.optimization_barrier((others, beside))
    return (part + others[0]) + (others[1] + others[2]), beside


def per_device(
    tokens, token_adapter_index, joined_weight_matrix, adapter_down_weight, adapter_up_weight
):
    owners = lax.axis_size("adapter")
    members = lax.axis_size("tensor")
    local_rows, width = tokens.shape
    group = members * local_rows
    held, rank, features = adapter_down_weight.shape
    columns = adapter_up_weight.shape[2]
    capacity = 4 * group // owners
    even = group // owners
    down = adapter_down_weight.reshape(held * rank, features)
    up = adapter_up_weight.reshape(held * rank, columns)
    wide = features + LANES

    order = jnp.arange(held, dtype=I32)
    started = scatter_start(jnp.concatenate([down, up], axis=1))

    gathered = lax.all_gather(tokens, "tensor", axis=0, tiled=True)
    ids = lax.all_gather(token_adapter_index, "tensor", axis=0, tiled=True)
    info, tall = plan(ids, owners, held, even)

    named = info[3, 0]
    started, away = lax.optimization_barrier((started, away_from(named)))
    piece = scatter_end(started, away)
    weights = lax.all_gather(piece, "adapter", axis=0, tiled=True)
    labels = scattered_order(named, held)

    here = lax.axis_index("tensor").astype(I32).reshape(1)
    send, rest_rows = route(here, info, gathered, features, owners, even, capacity)
    rows = exchange(send.reshape(owners, even, wide), "adapter")

    base = jnp.dot(gathered, joined_weight_matrix, preferred_element_type=F32)
    rows, base = lax.optimization_barrier((rows, base))

    rows = rows.reshape(owners * even, wide)
    low, _ = total_over_tensor(low_part(order, rows, down, rank))
    delta = delta_of(low, rows, up)
    places = jnp.broadcast_to(jnp.repeat(labels, rank)[None], (8, held * rank))
    said = rows.reshape(owners, even, wide)[:, 0, features + 3 : features + 6]
    rest_rows, delta, said, labels, places = lax.optimization_barrier(
        (rest_rows, delta, said, labels, places)
    )
    back = exchange(delta.reshape(owners, even, columns), "adapter").reshape(owners * even, columns)

    said = said.astype(I32)
    same = jnp.all(said[:, 0] == said[0, 0])
    full = jnp.where(same, said[0, 0], -1)
    largest = jnp.where(same, jnp.max(said[:, 1]), jnp.max(said[:, 2]))
    turns = (largest + even - 1) // even

    owner, place = info[0], info[2]

    def more(carry):
        turn, total = carry
        turn, source = lax.optimization_barrier((turn, gathered))
        wanted = (owner != full) & (place // even == turn)
        slot = jnp.where(wanted, owner * even + place % even, -1)
        chosen = (slot[None, :] == jnp.arange(owners * even, dtype=I32)[:, None]).astype(BF16)
        mine = lax.dynamic_slice_in_dim(source, here[0] * features, features, 1)
        numbers = jnp.pad(info[1][:, None].astype(BF16), ((0, 0), (1, LANES - 2)))
        mine = jnp.concatenate([mine, numbers], axis=1)
        moved = jnp.dot(chosen, mine, preferred_element_type=F32).astype(BF16)
        moved = exchange(moved.reshape(owners, even, wide), "adapter").reshape(owners * even, wide)
        more_low, _ = total_over_tensor(low_part(order, moved, down, rank))
        more_delta = delta_of(more_low, moved, up).reshape(owners, even, columns)
        more_back = exchange(more_delta, "adapter").reshape(owners * even, columns)
        return turn + 1, total + jnp.dot(chosen.T, more_back, preferred_element_type=F32)

    _, base = lax.while_loop(lambda carry: carry[0] < turns, more, (jnp.int32(1), base))


    rest_low, back = total_over_tensor(low_part(labels, rest_rows, weights, rank), back)
    return finish(full.reshape(1), places, tall, rest_low, rest_rows, base, back, weights, even)


def solution(mesh):
    return jax.shard_map(
        per_device,
        mesh=mesh,
        in_specs=(
            P(("adapter", "tensor"), None),
            P(("adapter", "tensor")),
            P(None, "tensor"),
            P("adapter", None, "tensor"),
            P("adapter", None, "tensor"),
        ),
        out_specs=P("adapter", "tensor"),
        check_vma=False,
    )
```
